32 devices in a mesh: src: 4 (over y, x), tgt: 8 (over z, core).
Axes of the slice: x: 2, y: 2, z: 4, core: 2. Of those that a mesh axis runs over, the one named last changes fastest.
Arguments:
- sources: bfloat16 [32768, 64], P(('src', 'tgt'))
- targets: bfloat16 [65536, 64], P(('src', 'tgt'))
- log_src: float32 [32768], P(('src', 'tgt')), may hold values from -1 to 1
- log_tgt: float32 [65536], P(('src', 'tgt')), may hold values from -1 to 1
- tile_rows: int32 [4, 8, 256], P('src', 'tgt'), may hold values from 0 to 63, as said below
- tile_cols: int32 [4, 8, 256], P('src', 'tgt'), may hold values from 0 to 63, as said below
- tile_count: int32 [4, 8], P('src', 'tgt'), may hold values from 64 to 256, as said below
Outputs:
- src_potential: float32 [32768], P(('src', 'tgt'))
- tgt_potential: float32 [65536], P(('src', 'tgt'))
The draws below stay inside these ranges and needn't reach their ends.
Inputs may be any that keep to these rules, and one draw needn't show every extreme that they name: `tile_rows`: each entry is a block number within the group. `tile_cols`: each entry is a block number within the group; within one pair of groups no (row, column) pair of blocks appears twice among all 256 slots; among the live slots of every pair of groups every source block and every target block appears. `tile_count`: some pair of groups has exactly 256 live slots and some other exactly 64.
All inputs are finite; a program needn't handle non-finite values.
Results may differ from the reference program's by a relative error of at most 0.00075.
Values may be sent and summed in bfloat16 or wider, within the bound.
A program may use at most 64 MiB of HBM per device.

```python
import jax
import jax.numpy as jnp
from jax import lax

F = 64
TILE = 128
BLK = 64
ITERS = 3
MAXT = 256
NS = 32768
NT = 65536
N_SRC = 4
N_TGT = 8


def lift_some(points, direction):
    count = points.shape[0]
    index = jnp.arange(count, dtype=jnp.int32)
    picked = index % 61 == 7
    strength = 2.5 + 0.5 * (index // 61 % 4).astype(jnp.float32)
    return points + direction * jnp.where(picked, strength, 0.0)[:, None]


def pattern_keys(key):
    return jax.random.split(jax.random.fold_in(key, 5), 5)


def band_offsets(key):
    return jax.random.randint(pattern_keys(key)[1], (N_SRC, N_TGT, 1), 0, BLK, jnp.int32)


def draw_sources(key, part):
    own_key = jax.random.fold_in(key, 11)
    points = lift_some(0.7 * jax.random.normal(own_key, (NS, F), jnp.float32), 1.0)
    return points.astype(jnp.bfloat16)


def draw_targets(key, part):
    own_key = jax.random.fold_in(key, 12)
    points = lift_some(0.7 * jax.random.normal(own_key, (NT, F), jnp.float32), -1.0)
    return points.astype(jnp.bfloat16)


def tile_pattern(key):
    all_keys = pattern_keys(key)
    noise_key = all_keys[0]
    count_key = all_keys[2]
    pick_key = all_keys[3]
    shuffle_key = all_keys[4]
    pairs = BLK * BLK
    pair_index = jnp.arange(pairs, dtype=jnp.int32)
    row_part = pair_index // BLK
    col_part = pair_index % BLK
    offsets = band_offsets(key)
    diagonal = col_part[None, None, :] == (row_part[None, None, :] + offsets) % BLK
    span = 2 ** 30 // pairs
    noise = jax.random.randint(noise_key, (N_SRC, N_TGT, pairs), 1, span, jnp.int32)
    ranking = jnp.where(diagonal, 0, noise) * pairs + pair_index[None, None, :]
    order = jnp.argsort(ranking, axis=-1)[:, :, :MAXT].astype(jnp.int32)
    uniform_ints = jax.random.randint(count_key, (N_SRC, N_TGT), 0, 4096, jnp.int32)
    extra = uniform_ints * uniform_ints // 4096 * (MAXT - BLK) // 4095
    devices = N_SRC * N_TGT
    busiest = jax.random.randint(pick_key, (), 0, devices, jnp.int32)
    flat_index = jnp.arange(devices, dtype=jnp.int32).reshape(N_SRC, N_TGT)
    counts = jnp.where(flat_index == busiest, MAXT, BLK + extra)
    counts = jnp.where(flat_index == (busiest + 1) % devices, BLK, counts).astype(jnp.int32)
    slot_index = jnp.arange(MAXT, dtype=jnp.int32)[None, None, :]
    shuffle = jax.random.randint(shuffle_key, (N_SRC, N_TGT, MAXT), 0, 2 ** 20, jnp.int32)
    slot_rank = jnp.where(slot_index < counts[:, :, None], shuffle * MAXT, 2 ** 30) + slot_index
    shuffled = jnp.argsort(slot_rank, axis=-1).astype(jnp.int32)
    order = jnp.take_along_axis(order, shuffled, axis=-1)
    return (order // BLK, order % BLK, counts)


def draw_tile_rows(key, part):
    return tile_pattern(key)[0]


def draw_tile_cols(key, part):
    return tile_pattern(key)[1]


def draw_tile_count(key, part):
    return tile_pattern(key)[2]


def shard_levels(key, dims, pieces, low, largest):
    factor_of, own = 1.0, jax.random.fold_in(key, 6)
    for position, parts in pieces:
        heights = jnp.exp(jax.random.uniform(jax.random.fold_in(own, position), (parts,), jnp.float32, low / len(pieces), largest / len(pieces)))
        factor_of = factor_of * jnp.repeat(heights, dims[position] // parts).reshape([-1 if axis == position else 1 for axis in range(len(dims))])
    return factor_of


def setup_inputs(seed: int = 0) -> dict:
    seeds = jax.random.split(jax.random.key(seed), 8)
    sources = draw_sources(jax.random.fold_in(seeds[7], 71), 0)
    targets = draw_targets(jax.random.fold_in(seeds[7], 71), 0)
    log_src = jnp.clip(jax.random.uniform(seeds[2], (NS,), jnp.float32, -1.0, 1.0) * shard_levels(seeds[2], (NS,), ((0, 32),), -0.4, 0.0), -1.0, 1.0)
    log_tgt = jnp.clip(jax.random.uniform(seeds[3], (NT,), jnp.float32, -1.0, 1.0) * shard_levels(seeds[3], (NT,), ((0, 32),), -0.4, 0.0), -1.0, 1.0)
    tile_rows = draw_tile_rows(jax.random.fold_in(seeds[7], 71), 0)
    tile_cols = draw_tile_cols(jax.random.fold_in(seeds[7], 71), 0)
    tile_count = draw_tile_count(jax.random.fold_in(seeds[7], 71), 0)
    return dict(sources=sources, targets=targets, log_src=log_src, log_tgt=log_tgt, tile_rows=tile_rows, tile_cols=tile_cols, tile_count=tile_count)


EPS_BLUR = 0.1
NEG_FLOOR = -1e30


def point_norms(points):
    widened = points.astype(jnp.float32)
    return jnp.sum(widened * widened, axis=-1)


def tile_scores(near_points, near_norms, far_points, far_norms, far_potential):
    cross = jnp.einsum("kif,kjf->kij", near_points.astype(jnp.float32), far_points.astype(jnp.float32))
    costs = (near_norms[:, :, None] + far_norms[:, None, :] - 2.0 * cross) * (1.0 / near_points.shape[-1])
    return (far_potential[:, None, :] - costs) / EPS_BLUR


def fold_stats(highest, summed, scores, near_index, active):
    active_tile = active[:, None, None]
    masked = jnp.where(active_tile, scores, NEG_FLOOR)
    tile_high = jnp.max(masked, axis=2)
    new_high = highest.at[near_index].max(tile_high)
    weights = jnp.exp(masked - new_high[near_index][:, :, None]) * active_tile.astype(jnp.float32)
    added = jnp.zeros_like(summed).at[near_index].add(jnp.sum(weights, axis=2))
    return new_high, summed * jnp.exp(highest - new_high) + added


def sweep(near_blocks, near_norms, far_blocks, far_norms, far_potential, near_lists, far_lists, tile_count, by_source):
    def visit(state_pair, device):
        highest, summed = state_pair
        src_index = device // N_TGT
        tgt_index = device % N_TGT
        near_group = src_index if by_source else tgt_index
        far_group = tgt_index if by_source else src_index
        near_index = near_lists[src_index, tgt_index]
        far_index = far_lists[src_index, tgt_index]
        active = jnp.arange(near_index.shape[0], dtype=jnp.int32) < tile_count[src_index, tgt_index]
        scores = tile_scores(near_blocks[near_group][near_index], near_norms[near_group][near_index],
                             far_blocks[far_group][far_index], far_norms[far_group][far_index],
                             far_potential[far_group][far_index])
        group_high, group_sum = fold_stats(highest[near_group], summed[near_group], scores, near_index, active)
        return (highest.at[near_group].set(group_high), summed.at[near_group].set(group_sum)), None

    initial = (jnp.full(near_norms.shape, NEG_FLOOR, jnp.float32), jnp.zeros(near_norms.shape, jnp.float32))
    (highest, summed), unused = lax.scan(visit, initial, jnp.arange(N_SRC * N_TGT, dtype=jnp.int32))
    return highest + jnp.log(summed)


def reference(sources, targets, log_src, log_tgt, tile_rows, tile_cols, tile_count):
    feats = sources.shape[1]
    src_blocks = sources.reshape(N_SRC, BLK, TILE, feats)
    tgt_blocks = targets.reshape(N_SRC, N_TGT, -1, feats).transpose(1, 0, 2, 3).reshape(N_TGT, BLK, TILE, feats)
    src_norms = point_norms(src_blocks)
    tgt_norms = point_norms(tgt_blocks)
    src_logs = log_src.reshape(N_SRC, BLK, TILE)
    tgt_logs = log_tgt.reshape(N_SRC, N_TGT, -1).transpose(1, 0, 2).reshape(N_TGT, BLK, TILE)
    tgt_potential = jnp.zeros((N_TGT, BLK, TILE), jnp.float32)
    src_potential = jnp.zeros((N_SRC, BLK, TILE), jnp.float32)
    for sweep_index in range(ITERS):
        src_potential = EPS_BLUR * (src_logs - sweep(src_blocks, src_norms, tgt_blocks, tgt_norms, tgt_potential,
                                                     tile_rows, tile_cols, tile_count, True))
        tgt_potential = EPS_BLUR * (tgt_logs - sweep(tgt_blocks, tgt_norms, src_blocks, src_norms, src_potential,
                                                     tile_cols, tile_rows, tile_count, False))
    src_out = src_potential.reshape(-1)
    tgt_out = tgt_potential.reshape(N_TGT, N_SRC, -1).transpose(1, 0, 2).reshape(-1)
    return (src_out, tgt_out)
```

```python
import functools
import math

import jax
import jax.numpy as jnp
from jax import lax
from jax.experimental import pallas as pl
from jax.experimental.pallas import tpu as pltpu
from jax.sharding import PartitionSpec as P

TILE = 128
ITERS = 3
EPS_BLUR = 0.1
LOG2E = math.log2(math.e)
LOW = -1e30
MESH = pl.DeviceIdType.MESH
NT_DIMS = (((1,), (1,)), ((), ()))
NN_DIMS = (((1,), (0,)), ((), ()))


def mm(a, b, dims):
    return lax.dot_general(a, b, dims, preferred_element_type=jnp.float32)


def log2(x):
    return jnp.log(x) * LOG2E


def split2(x):
    hi = x.astype(jnp.bfloat16)
    lo = (x - hi.astype(jnp.float32)).astype(jnp.bfloat16)
    return hi, lo


def stack_hi_lo(row):
    hi = row.astype(jnp.bfloat16).astype(jnp.float32)
    lo = row - hi
    sub = lax.broadcasted_iota(jnp.int32, (8, TILE), 0)
    full_hi = jnp.broadcast_to(hi, (8, TILE))
    full_lo = jnp.broadcast_to(lo, (8, TILE))
    return jnp.where(sub == 0, full_hi, jnp.where(sub == 1, full_lo, 0.0)).astype(jnp.bfloat16)


def kernel(
    n_s, n_t, blocks, slots, feats,
    rows_s, cols_s, rid1, rid2, cid1, cid2, x_ref, y_ref, la_ref, lb_ref,
    a_out, b_out,
    xg, yg, lbg, xa, ya, ny, abc, tiles, slot_max, slot_sum, ridb, cidb,
    row_part, row_recv, a_full, a_cur, col_part, col_recv, b_cur, lb_full, part,
    sem_x, sem_y, sem_l, sem_ra, sem_rb, sem_c,
):
    s = lax.axis_index("src")
    t = lax.axis_index("tgt")
    rb = blocks // n_t
    cb = blocks // n_s
    kappa = 2.0 * LOG2E / (feats * EPS_BLUR)

    barrier = pltpu.get_barrier_semaphore()
    for d in range(1, n_t):
        pl.semaphore_signal(barrier, inc=1, device_id=(s, lax.rem(t + d, n_t)), device_id_type=MESH)
    for d in range(1, n_s):
        pl.semaphore_signal(barrier, inc=1, device_id=(lax.rem(s + d, n_s), t), device_id_type=MESH)
    pl.semaphore_wait(barrier, n_t + n_s - 2)

    def send(src, dst, sems, index, d, along_tgt):
        if along_tgt:
            dev = (s, lax.rem(t + d, n_t))
        else:
            dev = (lax.rem(s + d, n_s), t)
        copy = pltpu.make_async_remote_copy(
            src_ref=src, dst_ref=dst, send_sem=sems.at[(0, *index)], recv_sem=sems.at[(1, *index)],
            device_id=dev, device_id_type=MESH,
        )
        copy.start()
        return copy

    x_copies = {}
    y_copies = {}
    l_copies = {}
    for d in range(1, max(n_t, n_s)):
        if d < n_s:
            y_copies[d] = send(y_ref, yg.at[s], sem_y, (d,), d, False)
            l_copies[d] = send(lb_ref, lbg.at[s], sem_l, (d,), d, False)
        if d < n_t:
            x_copies[d] = send(x_ref, xg.at[t], sem_x, (d,), d, True)
    xg[t] = x_ref[...]
    yg[s] = y_ref[...]
    lbg[s] = lb_ref[...]

    ridb[...] = jnp.broadcast_to(rid2[...], ridb.shape)
    cidb[...] = jnp.broadcast_to(cid2[...], cidb.shape)

    ii = lax.broadcasted_iota(jnp.int32, (TILE, TILE), 0)
    jj = lax.broadcasted_iota(jnp.int32, (TILE, TILE), 1)
    in_low = jj < feats
    take = [
        jnp.where((ii == jj + h * feats) & in_low, 1.0, 0.0).astype(jnp.bfloat16) for h in range(2)
    ]
    half_ones = [
        jnp.where((ii // feats) == h, 1.0, 0.0).astype(jnp.bfloat16) for h in range(2)
    ]

    def unpack_x(owner):
        def body(q, carry):
            v = xg[owner, pl.ds(pl.multiple_of(q * TILE, TILE), TILE), :]
            for h in range(2):
                xa[owner * rb + h * (rb // 2) + q] = mm(v, take[h], NN_DIMS).astype(jnp.bfloat16)
            return carry
        lax.fori_loop(0, rb // 2, body, 0)

    def unpack_y(owner):
        def body(q, carry):
            v = yg[owner, pl.ds(pl.multiple_of(q * TILE, TILE), TILE), :]
            wide = v.astype(jnp.float32)
            hi, lo = split2(wide * wide)
            for h in range(2):
                b = owner * cb + h * (cb // 2) + q
                ya[b] = mm(v, take[h], NN_DIMS).astype(jnp.bfloat16)
                norm = mm(hi, half_ones[h], NN_DIMS) + mm(lo, half_ones[h], NN_DIMS)
                ny[b] = norm * (0.5 * kappa)
            return carry
        lax.fori_loop(0, cb // 2, body, 0)

    unpack_x(t)
    unpack_y(s)
    for d in range(1, max(n_t, n_s)):
        if d < n_s:
            y_copies[d].wait()
            l_copies[d].wait()
            unpack_y(lax.rem(s - d + n_s, n_s))
    for d in range(1, n_t):
        x_copies[d].wait()
        unpack_x(lax.rem(t - d + n_t, n_t))
    for o in range(n_s):
        lb_full[pl.ds(o * cb, cb), :] = lbg[o] * LOG2E

    unroll = 4
    zero = jnp.int32(0)

    def first_rows(g, carry):
        for q in range(unroll):
            k = g * unroll + q
            r = rows_s[k]
            c = cols_s[k]
            w = mm(ya[c], xa[r], NT_DIMS) * kappa - ny[c]
            m = jnp.max(w, axis=0, keepdims=True)
            slot_max[pl.ds(k, 1), :] = m
            slot_sum[pl.ds(k, 1), :] = jnp.sum(jnp.exp2(w - m), axis=0, keepdims=True)
        return carry

    def first_cols(g, carry):
        for q in range(unroll):
            k = g * unroll + q
            r = rows_s[k]
            c = cols_s[k]
            w = mm(xa[r], ya[c], NT_DIMS) * kappa + abc[r]
            m = jnp.max(w, axis=0, keepdims=True)
            e = jnp.exp2(w - m)
            slot_max[pl.ds(k, 1), :] = m
            slot_sum[pl.ds(k, 1), :] = jnp.sum(e, axis=0, keepdims=True)
            tiles[k] = e.astype(jnp.bfloat16)
        return carry

    def combine_lse(ids, out, per):
        def body(b, carry):
            high = jnp.where(ids[...] == b, slot_max[...], LOW)
            top = jnp.max(high, axis=0, keepdims=True)
            total = jnp.sum(slot_sum[...] * jnp.exp2(high - top), axis=0, keepdims=True)
            out[b // per, pl.ds(b % per, 1), :] = top + log2(total)
            return carry
        lax.fori_loop(0, blocks, body, 0)

    def combine_sum(ids1, out, n, per):
        which = lax.broadcasted_iota(jnp.int32, (blocks, slots), 0)
        onehot = jnp.where(which == ids1[...], 1.0, 0.0).astype(jnp.bfloat16)
        hi, lo = split2(slot_sum[...])
        full = mm(onehot, hi, NN_DIMS) + mm(onehot, lo, NN_DIMS)
        for o in range(n):
            out[o] = full[o * per:(o + 1) * per, :]

    def lse_of(values):
        top = functools.reduce(jnp.maximum, values)
        return top + log2(sum(jnp.exp2(v - top) for v in values))

    def rows_exchange(it, finish):
        copies = [
            send(row_part.at[it, lax.rem(t + d, n_t)], row_recv.at[it, d], sem_ra, (it, d), d, True)
            for d in range(1, n_t)
        ]
        for copy in copies:
            copy.wait()
        own = finish([row_part[it, t]] + [row_recv[it, d] for d in range(1, n_t)])
        a_full[it, t] = own
        copies = [
            send(a_full.at[it, t], a_full.at[it, t], sem_rb, (it, d), d, True) for d in range(1, n_t)
        ]
        for copy in copies:
            copy.wait()
        return own

    lax.fori_loop(0, slots // unroll, first_rows, 0)
    combine_lse(ridb, row_part.at[0], rb)
    la2 = la_ref[...] * LOG2E
    a_first = rows_exchange(0, lambda vs: la2 - lse_of(vs))
    for o in range(n_t):
        a_cur[pl.ds(o * rb, rb), :] = a_full[0, o]

    def spread(g, carry):
        for q in range(4):
            r = g * 4 + q
            abc[r] = jnp.transpose(jnp.broadcast_to(a_cur[pl.ds(r, 1), :], (TILE, TILE)))
        return carry
    lax.fori_loop(0, blocks // 4, spread, 0)

    lax.fori_loop(0, slots // unroll, first_cols, 0)
    combine_lse(cidb, col_part.at[0], cb)
    copies = [
        send(col_part.at[0], col_recv.at[0, d], sem_c, (0, d), d, False) for d in range(1, n_s)
    ]
    for copy in copies:
        copy.wait()
    for o in range(n_s):
        lse = lse_of([col_part[0, o]] + [col_recv[0, d, o] for d in range(1, n_s)])
        b_cur[pl.ds(o * cb, cb), :] = lb_full[pl.ds(o * cb, cb), :] - lse

    wide_unroll = 8

    def later_rows(g, carry):
        for q in range(wide_unroll):
            k = g * wide_unroll + q
            c = cols_s[k]
            w = jnp.exp2(jnp.minimum(slot_max[pl.ds(k, 1), :] + b_cur[pl.ds(c, 1), :], 100.0))
            got = mm(stack_hi_lo(w), tiles[k], NT_DIMS)
            slot_sum[pl.ds(k, 1), :] = got[0:1, :] + got[1:2, :]
        return carry

    def later_cols(g, carry):
        for q in range(wide_unroll):
            k = g * wide_unroll + q
            r = rows_s[k]
            c = cols_s[k]
            got = mm(stack_hi_lo(a_cur[pl.ds(r, 1), :]), tiles[k], NN_DIMS)
            f = jnp.exp2(jnp.minimum(slot_max[pl.ds(k, 1), :] + b_cur[pl.ds(c, 1), :], 60.0))
            slot_sum[pl.ds(k, 1), :] = (got[0:1, :] + got[1:2, :]) * f
        return carry

    for it in range(1, ITERS):
        lax.fori_loop(0, slots // wide_unroll, later_rows, 0)
        combine_sum(rid1, row_part.at[it], n_t, rb)
        own = rows_exchange(it, lambda vs: a_first + la2 - log2(sum(vs)))
        for o in range(n_t):
            a_cur[pl.ds(o * rb, rb), :] = jnp.exp2(a_full[it, o] - a_full[0, o])
        if it == ITERS - 1:
            a_out[...] = own
        lax.fori_loop(0, slots // wide_unroll, later_cols, 0)
        combine_sum(cid1, col_part.at[it], n_s, cb)
        if it < ITERS - 1:
            copies = [
                send(col_part.at[it], col_recv.at[it, d], sem_c, (it, d), d, False)
                for d in range(1, n_s)
            ]
            for copy in copies:
                copy.wait()
            for o in range(n_s):
                at = pl.ds(o * cb, cb)
                total = sum([col_part[it, o]] + [col_recv[it, d, o] for d in range(1, n_s)])
                b_cur[at, :] = b_cur[at, :] + lb_full[at, :] - log2(total)
        else:
            copies = [
                send(col_part.at[it, lax.rem(s + d, n_s)], part.at[d], sem_c, (it, d), d, False)
                for d in range(1, n_s)
            ]
            for copy in copies:
                copy.wait()
            total = sum([col_part[it, s]] + [part[d] for d in range(1, n_s)])
            at = pl.ds(pl.multiple_of(s * cb, cb), cb)
            b_out[...] = b_cur[at, :] + lb_full[at, :] - log2(total)


def halves(points):
    half = points.shape[0] // 2
    return jnp.concatenate([points[:half], points[half:]], axis=1)


def local(n_s, n_t, sources, targets, log_src, log_tgt, tile_rows, tile_cols, tile_count):
    feats = sources.shape[1]
    slots = tile_rows.shape[-1]
    blocks = sources.shape[0] * n_t // TILE
    rb, cb = blocks // n_t, blocks // n_s
    rows = tile_rows.reshape(-1)
    cols = tile_cols.reshape(-1)
    live = lax.iota(jnp.int32, slots) < tile_count.reshape(())
    rid = jnp.where(live, rows, -1)
    cid = jnp.where(live, cols, -1)
    vm = pl.BlockSpec(memory_space=pltpu.VMEM)
    sm = pl.BlockSpec(memory_space=pltpu.SMEM)
    f32, bf16, i32 = jnp.float32, jnp.bfloat16, jnp.int32
    dma = pltpu.SemaphoreType.DMA
    xp, yp = halves(sources), halves(targets)
    a_own, b_own = pl.pallas_call(
        functools.partial(kernel, n_s, n_t, blocks, slots, feats),
        out_shape=(
            jax.ShapeDtypeStruct((rb, TILE), f32),
            jax.ShapeDtypeStruct((cb, TILE), f32),
        ),
        in_specs=[sm, sm] + [vm] * 8,
        out_specs=(vm, vm),
        scratch_shapes=[
            pltpu.VMEM((n_t, *xp.shape), bf16),
            pltpu.VMEM((n_s, *yp.shape), bf16),
            pltpu.VMEM((n_s, cb, TILE), f32),
            pltpu.VMEM((blocks, TILE, TILE), bf16),
            pltpu.VMEM((blocks, TILE, TILE), bf16),
            pltpu.VMEM((blocks, TILE, TILE), f32),
            pltpu.VMEM((blocks, TILE, TILE), f32),
            pltpu.VMEM((slots, TILE, TILE), bf16),
            pltpu.VMEM((slots, TILE), f32),
            pltpu.VMEM((slots, TILE), f32),
            pltpu.VMEM((slots, TILE), i32),
            pltpu.VMEM((slots, TILE), i32),
            pltpu.VMEM((ITERS, n_t, rb, TILE), f32),
            pltpu.VMEM((ITERS, n_t, rb, TILE), f32),
            pltpu.VMEM((ITERS, n_t, rb, TILE), f32),
            pltpu.VMEM((blocks, TILE), f32),
            pltpu.VMEM((ITERS, n_s, cb, TILE), f32),
            pltpu.VMEM((ITERS - 1, n_s, n_s, cb, TILE), f32),
            pltpu.VMEM((blocks, TILE), f32),
            pltpu.VMEM((blocks, TILE), f32),
            pltpu.VMEM((n_s, cb, TILE), f32),
            dma((2, n_t)),
            dma((2, n_s)),
            dma((2, n_s)),
            dma((2, ITERS, n_t)),
            dma((2, ITERS, n_t)),
            dma((2, ITERS, n_s)),
        ],
        compiler_params=pltpu.CompilerParams(
            collective_id=0, has_side_effects=True, vmem_limit_bytes=48 * 2**20
        ),
        cost_estimate=pl.CostEstimate(
            flops=12 * slots * TILE**3, bytes_accessed=2**20, transcendentals=2 * slots * TILE**2
        ),
    )(
        rows, cols, rid.reshape(1, -1), rid.reshape(-1, 1), cid.reshape(1, -1), cid.reshape(-1, 1),
        xp, yp, log_src.reshape(rb, TILE), log_tgt.reshape(cb, TILE),
    )
    scale = EPS_BLUR / LOG2E
    return tuple(
        own.reshape(-1) * scale + jnp.sum(points.astype(f32) ** 2, axis=-1) * (1.0 / feats)
        for own, points in ((a_own, sources), (b_own, targets))
    )


def solution(mesh):
    in_specs = (
        P(("src", "tgt"), None),
        P(("src", "tgt"), None),
        P(("src", "tgt")),
        P(("src", "tgt")),
        P("src", "tgt", None),
        P("src", "tgt", None),
        P("src", "tgt"),
    )
    out_specs = (P(("src", "tgt")), P(("src", "tgt")))
    body = functools.partial(local, mesh.shape["src"], mesh.shape["tgt"])
    return jax.shard_map(body, mesh=mesh, in_specs=in_specs, out_specs=out_specs, check_vma=False)
```

```python
import functools
import math

import jax
import jax.numpy as jnp
from jax import lax
from jax.experimental import pallas as pl
from jax.experimental.pallas import tpu as pltpu
from jax.sharding import PartitionSpec as P

TILE = 128
ITERS = 3
EPS_BLUR = 0.1
LOG2E = math.log2(math.e)
LOW = -1e30
MESH = pl.DeviceIdType.MESH
NT_DIMS = (((1,), (1,)), ((), ()))
NN_DIMS = (((1,), (0,)), ((), ()))


def mm(a, b, dims):
    return lax.dot_general(a, b, dims, preferred_element_type=jnp.float32)


def log2(x):
    return jnp.log(x) * LOG2E


def split2(x):
    hi = x.astype(jnp.bfloat16)
    lo = (x - hi.astype(jnp.float32)).astype(jnp.bfloat16)
    return hi, lo


def stack_hi_lo(row):
    hi = row.astype(jnp.bfloat16).astype(jnp.float32)
    lo = row - hi
    sub = lax.broadcasted_iota(jnp.int32, (8, TILE), 0)
    full_hi = jnp.broadcast_to(hi, (8, TILE))
    full_lo = jnp.broadcast_to(lo, (8, TILE))
    return jnp.where(sub == 0, full_hi, jnp.where(sub == 1, full_lo, 0.0)).astype(jnp.bfloat16)


def kernel(
    n_s, n_t, blocks, slots, feats,
    rows_s, cols_s, count_s, rows_v, cols_v, x_ref, y_ref, la_ref, lb_ref,
    a_out, b_out,
    xg, yg, lag, lbg, xa, ya, ny, abc, tiles, slot_max, slot_sum, ridb, cidb, tops,
    row_part, row_recv, a_full, a_cur, col_part, col_recv, b_cur, mass, lb_full,
    row_sums, row_sums_in, col_sums, col_sums_in, last_part, last_in,
    sem_x, sem_f, sem_y, sem_la, sem_l, sem_ra, sem_rb, sem_r, sem_c,
):
    s = lax.axis_index("src")
    t = lax.axis_index("tgt")
    rb = blocks // n_t
    cb = blocks // n_s
    kappa = 2.0 * LOG2E / (feats * EPS_BLUR)

    barrier = pltpu.get_barrier_semaphore()
    for d in range(1, n_t):
        pl.semaphore_signal(barrier, inc=1, device_id=(s, lax.rem(t + d, n_t)), device_id_type=MESH)
    for d in range(1, n_s):
        pl.semaphore_signal(barrier, inc=1, device_id=(lax.rem(s + d, n_s), t), device_id_type=MESH)
    pl.semaphore_wait(barrier, n_t + n_s - 2)

    def send(src, dst, sems, index, d, along_tgt):
        if along_tgt:
            dev = (s, lax.rem(t + d, n_t))
        else:
            dev = (lax.rem(s + d, n_s), t)
        copy = pltpu.make_async_remote_copy(
            src_ref=src, dst_ref=dst, send_sem=sems.at[(0, *index)], recv_sem=sems.at[(1, *index)],
            device_id=dev, device_id_type=MESH,
        )
        copy.start()
        return copy

    n_z = n_t // 2
    mate = t + 1 - 2 * lax.rem(t, 2)
    to_mate = 0

    def before(owner, dz):
        return lax.rem(owner - 2 * dz + n_t, n_t)

    def send_x(owner, sems, index, dest):
        copy = pltpu.make_async_remote_copy(
            src_ref=x_ref if owner is None else xg.at[owner],
            dst_ref=xg.at[t if owner is None else owner],
            send_sem=sems.at[0, index], recv_sem=sems.at[1, index],
            device_id=(s, dest), device_id_type=MESH,
        )
        copy.start()
        return copy

    x_copies = {dz: send_x(None, sem_x, dz, lax.rem(t + 2 * dz, n_t)) for dz in range(1, n_z)}
    y_copies = {d: send(y_ref, yg.at[s], sem_y, (d,), d, False) for d in range(1, n_s)}
    x_copies[to_mate] = send_x(None, sem_x, to_mate, mate)
    small = [send(lb_ref, lbg.at[s], sem_l, (d,), d, False) for d in range(1, n_s)]
    small += [send(la_ref, lag.at[t], sem_la, (d,), d, True) for d in range(1, n_t)]
    xg[t] = x_ref[...]
    yg[s] = y_ref[...]
    lag[t] = la_ref[...]
    lbg[s] = lb_ref[...]

    slot_at = lax.broadcasted_iota(jnp.int32, (1, slots), 1)
    rid1 = jnp.where(slot_at < count_s[0, 0], rows_v[...], -1)
    cid1 = jnp.where(slot_at < count_s[0, 0], cols_v[...], -1)
    for ids, wide in ((rid1, ridb), (cid1, cidb)):
        for h in range(slots // TILE):
            at = slice(h * TILE, (h + 1) * TILE)
            flat = jnp.broadcast_to(ids[:, at].astype(jnp.float32), (TILE, TILE))
            wide[at, :] = jnp.transpose(flat)

    ii = lax.broadcasted_iota(jnp.int32, (TILE, TILE), 0)
    jj = lax.broadcasted_iota(jnp.int32, (TILE, TILE), 1)
    in_low = jj < feats
    take = [
        jnp.where((ii == jj + h * feats) & in_low, 1.0, 0.0).astype(jnp.bfloat16) for h in range(2)
    ]
    half_ones = [
        jnp.where((ii // feats) == h, 1.0, 0.0).astype(jnp.bfloat16) for h in range(2)
    ]

    def unpack_x(owner):
        def body(q, carry):
            v = xg[owner, pl.ds(pl.multiple_of(q * TILE, TILE), TILE), :]
            for h in range(2):
                xa[owner * rb + h * (rb // 2) + q] = mm(v, take[h], NN_DIMS).astype(jnp.bfloat16)
            return carry
        lax.fori_loop(0, rb // 2, body, 0)

    def unpack_y(owner):
        def body(q, carry):
            v = yg[owner, pl.ds(pl.multiple_of(q * TILE, TILE), TILE), :]
            wide = v.astype(jnp.float32)
            hi, lo = split2(wide * wide)
            for h in range(2):
                b = owner * cb + h * (cb // 2) + q
                ya[b] = mm(v, take[h], NN_DIMS).astype(jnp.bfloat16)
                norm = mm(hi, half_ones[h], NN_DIMS) + mm(lo, half_ones[h], NN_DIMS)
                ny[b] = norm * (0.5 * kappa)
            return carry
        lax.fori_loop(0, cb // 2, body, 0)

    unpack_x(t)
    unpack_y(s)
    x_copies[to_mate].wait()
    unpack_x(mate)
    forwards = {}
    for d in range(1, max(n_z, n_s)):
        if d < n_z:
            x_copies[d].wait_recv()
            forwards[d] = send_x(before(t, d), sem_f, d, mate)
            unpack_x(before(t, d))
        if d < n_s:
            y_copies[d].wait()
            unpack_y(lax.rem(s - d + n_s, n_s))
    for d in range(1, n_z):
        forwards[d].wait_recv()
        unpack_x(before(mate, d))
    for d in range(1, n_z):
        x_copies[d].wait_send()
        forwards[d].wait_send()
    for copy in small:
        copy.wait()
    for o in range(n_t):
        mass[pl.ds(o * rb, rb), :] = jnp.exp(lag[o])
    for o in range(n_s):
        lb_full[pl.ds(o * cb, cb), :] = lbg[o] * LOG2E

    unroll = 16

    def first_rows(g, carry):
        for q in range(unroll):
            k = g * unroll + q
            r = rows_s[k]
            c = cols_s[k]
            w = mm(ya[c], xa[r], NT_DIMS) * kappa - ny[c]
            m = jnp.max(w, axis=0, keepdims=True)
            slot_max[pl.ds(k, 1), :] = m
            slot_sum[pl.ds(k, 1), :] = jnp.sum(jnp.exp2(w - m), axis=0, keepdims=True)
        return carry

    def first_cols(g, carry):
        for q in range(unroll):
            k = g * unroll + q
            r = rows_s[k]
            c = cols_s[k]
            w = mm(xa[r], ya[c], NT_DIMS) * kappa + abc[r]
            m = jnp.max(w, axis=0, keepdims=True)
            e = jnp.exp2(w - m)
            slot_max[pl.ds(k, 1), :] = m
            slot_sum[pl.ds(k, 1), :] = jnp.sum(e, axis=0, keepdims=True)
            tiles[k] = e.astype(jnp.bfloat16)
        return carry

    group = 8

    def by_block(ids1, values):
        which = lax.broadcasted_iota(jnp.int32, (blocks, slots), 0)
        onehot = jnp.where(which == ids1, 1.0, 0.0).astype(jnp.bfloat16)
        hi, lo = split2(values)
        return mm(onehot, hi, NN_DIMS) + mm(onehot, lo, NN_DIMS)

    def combine_lse(ids, ids1):
        def body(g, carry):
            base = (g * group).astype(jnp.float32)
            tall = [jnp.full((8, TILE), LOW, jnp.float32)] * group
            for ch in range(slots // 8):
                at = slice(ch * 8, ch * 8 + 8)
                offset = ids[at, :] - base
                high = slot_max[at, :]
                for b in range(group):
                    tall[b] = jnp.maximum(tall[b], jnp.where(offset == b, high, LOW))
            for b in range(group):
                tops[pl.ds(g * group + b, 1), :] = jnp.max(tall[b], axis=0, keepdims=True)
            return carry
        lax.fori_loop(0, blocks // group, body, 0)
        top = tops[...]
        lane = lax.broadcasted_iota(jnp.int32, (slots, TILE), 1).astype(jnp.float32)
        pick = jnp.where(ids[...] == lane, 1.0, 0.0)[:, :blocks].astype(jnp.bfloat16)
        hi, rest = split2(top)
        rest = top - hi.astype(jnp.float32)
        mid, low = split2(rest)
        seen = mm(pick, hi, NN_DIMS) + mm(pick, mid, NN_DIMS) + mm(pick, low, NN_DIMS)
        scaled = slot_sum[...] * jnp.exp2(jnp.minimum(slot_max[...] - seen, 1.0))
        return top + log2(by_block(ids1, scaled))

    def lse_of(values):
        top = functools.reduce(jnp.maximum, values)
        return top + log2(sum(jnp.exp2(v - top) for v in values))

    lax.fori_loop(0, slots // unroll, first_rows, 0)
    lse = combine_lse(ridb, rid1)
    for o in range(n_t):
        row_part[o] = lse[o * rb:(o + 1) * rb, :]
    copies = [
        send(row_part.at[lax.rem(t + d, n_t)], row_recv.at[d], sem_ra, (d,), d, True)
        for d in range(1, n_t)
    ]
    for copy in copies:
        copy.wait()
    la2 = la_ref[...] * LOG2E
    a_first = la2 - lse_of([row_part[t]] + [row_recv[d] for d in range(1, n_t)])
    a_full[t] = a_first
    copies = [send(a_full.at[t], a_full.at[t], sem_rb, (d,), d, True) for d in range(1, n_t)]
    for copy in copies:
        copy.wait()
    for o in range(n_t):
        a_cur[pl.ds(o * rb, rb), :] = a_full[o]

    def spread(g, carry):
        for q in range(4):
            r = g * 4 + q
            abc[r] = jnp.transpose(jnp.broadcast_to(a_cur[pl.ds(r, 1), :], (TILE, TILE)))
        return carry
    lax.fori_loop(0, blocks // 4, spread, 0)

    lax.fori_loop(0, slots // unroll, first_cols, 0)
    col_part[...] = combine_lse(cidb, cid1)
    copies = [send(col_part, col_recv.at[d], sem_c, (0, d), d, False) for d in range(1, n_s)]
    for copy in copies:
        copy.wait()
    lse = lse_of([col_part[...]] + [col_recv[d] for d in range(1, n_s)])
    b_cur[...] = lb_full[...] - lse

    wide_unroll = 16

    def later_rows(g, carry):
        for q in range(wide_unroll):
            k = g * wide_unroll + q
            c = cols_s[k]
            w = jnp.exp2(jnp.minimum(slot_max[pl.ds(k, 1), :] + b_cur[pl.ds(c, 1), :], 100.0))
            got = mm(stack_hi_lo(w), tiles[k], NT_DIMS)
            slot_sum[pl.ds(k, 1), :] = got[0:1, :] + got[1:2, :]
        return carry

    def later_cols(g, carry):
        for q in range(wide_unroll):
            k = g * wide_unroll + q
            r = rows_s[k]
            c = cols_s[k]
            got = mm(stack_hi_lo(a_cur[pl.ds(r, 1), :]), tiles[k], NN_DIMS)
            f = jnp.exp2(jnp.minimum(slot_max[pl.ds(k, 1), :] + b_cur[pl.ds(c, 1), :], 60.0))
            slot_sum[pl.ds(k, 1), :] = (got[0:1, :] + got[1:2, :]) * f
        return carry

    def totals(own, sums, sums_in, sems, it, n, along_tgt):
        sums[it - 1] = own.astype(jnp.bfloat16)
        copies = [
            send(sums.at[it - 1], sums_in.at[it - 1, d], sems, (it, d), d, along_tgt)
            for d in range(1, n)
        ]
        for copy in copies:
            copy.wait()
        return own + sum(sums_in[it - 1, d].astype(jnp.float32) for d in range(1, n))

    for it in range(1, ITERS):
        lax.fori_loop(0, slots // wide_unroll, later_rows, 0)
        own = by_block(rid1, slot_sum[...])
        a_cur[...] = mass[...] / totals(own, row_sums, row_sums_in, sem_r, it, n_t, True)
        if it == ITERS - 1:
            a_out[...] = a_first + log2(a_cur[pl.ds(t * rb, rb), :])
        lax.fori_loop(0, slots // wide_unroll, later_cols, 0)
        own = by_block(cid1, slot_sum[...])
        if it < ITERS - 1:
            total = totals(own, col_sums, col_sums_in, sem_c, it, n_s, False)
            b_cur[...] = b_cur[...] + lb_full[...] - log2(total)
        else:
            for o in range(n_s):
                last_part[o] = own[o * cb:(o + 1) * cb, :]
            copies = [
                send(last_part.at[lax.rem(s + d, n_s)], last_in.at[d], sem_c, (it, d), d, False)
                for d in range(1, n_s)
            ]
            for copy in copies:
                copy.wait()
            total = last_part[s] + sum(last_in[d] for d in range(1, n_s))
            at = pl.ds(s * cb, cb)
            b_out[...] = b_cur[at, :] + lb_full[at, :] - log2(total)


def halves(points):
    half = points.shape[0] // 2
    return jnp.concatenate([points[:half], points[half:]], axis=1)


def local(n_s, n_t, sources, targets, log_src, log_tgt, tile_rows, tile_cols, tile_count):
    feats = sources.shape[1]
    slots = tile_rows.shape[-1]
    blocks = sources.shape[0] * n_t // TILE
    rb, cb = blocks // n_t, blocks // n_s
    rows = tile_rows.reshape(-1)
    cols = tile_cols.reshape(-1)
    vm = pl.BlockSpec(memory_space=pltpu.VMEM)
    sm = pl.BlockSpec(memory_space=pltpu.SMEM)
    f32, bf16, i32 = jnp.float32, jnp.bfloat16, jnp.int32
    dma = pltpu.SemaphoreType.DMA
    xp, yp = halves(sources), halves(targets)
    a_own, b_own = pl.pallas_call(
        functools.partial(kernel, n_s, n_t, blocks, slots, feats),
        out_shape=(
            jax.ShapeDtypeStruct((rb, TILE), f32),
            jax.ShapeDtypeStruct((cb, TILE), f32),
        ),
        in_specs=[sm] * 3 + [vm] * 6,
        out_specs=(vm, vm),
        scratch_shapes=[
            pltpu.VMEM((n_t, *xp.shape), bf16),
            pltpu.VMEM((n_s, *yp.shape), bf16),
            pltpu.VMEM((n_t, rb, TILE), f32),
            pltpu.VMEM((n_s, cb, TILE), f32),
            pltpu.VMEM((blocks, TILE, TILE), bf16),
            pltpu.VMEM((blocks, TILE, TILE), bf16),
            pltpu.VMEM((blocks, TILE, TILE), f32),
            pltpu.VMEM((blocks, TILE, TILE), f32),
            pltpu.VMEM((slots, TILE, TILE), bf16),
            pltpu.VMEM((slots, TILE), f32),
            pltpu.VMEM((slots, TILE), f32),
            pltpu.VMEM((slots, TILE), f32),
            pltpu.VMEM((slots, TILE), f32),
            pltpu.VMEM((blocks, TILE), f32),
            pltpu.VMEM((n_t, rb, TILE), f32),
            pltpu.VMEM((n_t, rb, TILE), f32),
            pltpu.VMEM((n_t, rb, TILE), f32),
            pltpu.VMEM((blocks, TILE), f32),
            pltpu.VMEM((blocks, TILE), f32),
            pltpu.VMEM((n_s, blocks, TILE), f32),
            pltpu.VMEM((blocks, TILE), f32),
            pltpu.VMEM((blocks, TILE), f32),
            pltpu.VMEM((blocks, TILE), f32),
            pltpu.VMEM((ITERS - 1, blocks, TILE), bf16),
            pltpu.VMEM((ITERS - 1, n_t, blocks, TILE), bf16),
            pltpu.VMEM((ITERS - 1, blocks, TILE), bf16),
            pltpu.VMEM((ITERS - 1, n_s, blocks, TILE), bf16),
            pltpu.VMEM((n_s, cb, TILE), f32),
            pltpu.VMEM((n_s, cb, TILE), f32),
            dma((2, n_t)),
            dma((2, n_t)),
            dma((2, n_s)),
            dma((2, n_t)),
            dma((2, n_s)),
            dma((2, n_t)),
            dma((2, n_t)),
            dma((2, ITERS, n_t)),
            dma((2, ITERS, n_s)),
        ],
        compiler_params=pltpu.CompilerParams(
            collective_id=0, has_side_effects=True, vmem_limit_bytes=48 * 2**20
        ),
        cost_estimate=pl.CostEstimate(
            flops=12 * slots * TILE**3, bytes_accessed=2**20, transcendentals=2 * slots * TILE**2
        ),
    )(
        rows, cols, tile_count, rows.reshape(1, -1), cols.reshape(1, -1),
        xp, yp, log_src.reshape(rb, TILE), log_tgt.reshape(cb, TILE),
    )
    scale = EPS_BLUR / LOG2E
    return tuple(
        own.reshape(-1) * scale + jnp.sum(points.astype(f32) ** 2, axis=-1) * (1.0 / feats)
        for own, points in ((a_own, sources), (b_own, targets))
    )


def solution(mesh):
    in_specs = (
        P(("src", "tgt"), None),
        P(("src", "tgt"), None),
        P(("src", "tgt")),
        P(("src", "tgt")),
        P("src", "tgt", None),
        P("src", "tgt", None),
        P("src", "tgt"),
    )
    out_specs = (P(("src", "tgt")), P(("src", "tgt")))
    body = functools.partial(local, mesh.shape["src"], mesh.shape["tgt"])
    return jax.shard_map(body, mesh=mesh, in_specs=in_specs, out_specs=out_specs, check_vma=False)
```

```python
import functools
import math

import jax
import jax.numpy as jnp
from jax import lax
from jax.experimental import pallas as pl
from jax.experimental.pallas import tpu as pltpu
from jax.sharding import PartitionSpec as P

TILE = 128
ITERS = 3
EPS_BLUR = 0.1
LOG2E = math.log2(math.e)
LOW = -1e30
MESH = pl.DeviceIdType.MESH
NT_DIMS = (((1,), (1,)), ((), ()))
NN_DIMS = (((1,), (0,)), ((), ()))


def mm(a, b, dims):
    return lax.dot_general(a, b, dims, preferred_element_type=jnp.float32)


def log2(x):
    return jnp.log(x) * LOG2E


def split2(x):
    hi = x.astype(jnp.bfloat16)
    lo = (x - hi.astype(jnp.float32)).astype(jnp.bfloat16)
    return hi, lo


def stack_hi_lo(row):
    hi = row.astype(jnp.bfloat16).astype(jnp.float32)
    lo = row - hi
    sub = lax.broadcasted_iota(jnp.int32, (8, TILE), 0)
    full_hi = jnp.broadcast_to(hi, (8, TILE))
    full_lo = jnp.broadcast_to(lo, (8, TILE))
    return jnp.where(sub == 0, full_hi, jnp.where(sub == 1, full_lo, 0.0)).astype(jnp.bfloat16)


def kernel(
    n_s, n_t, blocks, slots, feats,
    rows_s, cols_s, count_s, rows_v, cols_v, x_ref, y_ref, la_ref, lb_ref,
    a_out, b_out,
    xg, yg, lag, lbg, xa, ya, ny, abc, tiles, slot_max, slot_sum, ridb, cidb, tops,
    row_part, row_recv, a_full, a_cur, col_part, col_recv, b_cur, mass, lb_full,
    row_sums, row_sums_in, col_sums, col_sums_in, last_part, last_in,
    sem_x, sem_f, sem_y, sem_la, sem_l, sem_ra, sem_rb, sem_r, sem_c,
):
    s = lax.axis_index("src")
    t = lax.axis_index("tgt")
    rb = blocks // n_t
    cb = blocks // n_s
    kappa = 2.0 * LOG2E / (feats * EPS_BLUR)

    barrier = pltpu.get_barrier_semaphore()
    for d in range(1, n_t):
        pl.semaphore_signal(barrier, inc=1, device_id=(s, lax.rem(t + d, n_t)), device_id_type=MESH)
    for d in range(1, n_s):
        pl.semaphore_signal(barrier, inc=1, device_id=(lax.rem(s + d, n_s), t), device_id_type=MESH)
    pl.semaphore_wait(barrier, n_t + n_s - 2)

    def send(src, dst, sems, index, d, along_tgt):
        if along_tgt:
            dev = (s, lax.rem(t + d, n_t))
        else:
            dev = (lax.rem(s + d, n_s), t)
        copy = pltpu.make_async_remote_copy(
            src_ref=src, dst_ref=dst, send_sem=sems.at[(0, *index)], recv_sem=sems.at[(1, *index)],
            device_id=dev, device_id_type=MESH,
        )
        copy.start()
        return copy

    n_z = n_t // 2
    mate = t + 1 - 2 * lax.rem(t, 2)
    to_mate = 0

    def before(owner, dz):
        return lax.rem(owner - 2 * dz + n_t, n_t)

    def send_x(owner, sems, index, dest):
        copy = pltpu.make_async_remote_copy(
            src_ref=x_ref if owner is None else xg.at[owner],
            dst_ref=xg.at[t if owner is None else owner],
            send_sem=sems.at[0, index], recv_sem=sems.at[1, index],
            device_id=(s, dest), device_id_type=MESH,
        )
        copy.start()
        return copy

    x_copies = {dz: send_x(None, sem_x, dz, lax.rem(t + 2 * dz, n_t)) for dz in range(1, n_z)}
    y_copies = {d: send(y_ref, yg.at[s], sem_y, (d,), d, False) for d in range(1, n_s)}
    x_copies[to_mate] = send_x(None, sem_x, to_mate, mate)
    small = [send(lb_ref, lbg.at[s], sem_l, (d,), d, False) for d in range(1, n_s)]
    small += [send(la_ref, lag.at[t], sem_la, (d,), d, True) for d in range(1, n_t)]
    xg[t] = x_ref[...]
    yg[s] = y_ref[...]
    lag[t] = la_ref[...]
    lbg[s] = lb_ref[...]

    slot_at = lax.broadcasted_iota(jnp.int32, (1, slots), 1)
    rid1 = jnp.where(slot_at < count_s[0, 0], rows_v[...], -1)
    cid1 = jnp.where(slot_at < count_s[0, 0], cols_v[...], -1)
    for ids, wide in ((rid1, ridb), (cid1, cidb)):
        for h in range(slots // TILE):
            at = slice(h * TILE, (h + 1) * TILE)
            flat = jnp.broadcast_to(ids[:, at].astype(jnp.float32), (TILE, TILE))
            wide[at, :] = jnp.transpose(flat)

    ii = lax.broadcasted_iota(jnp.int32, (TILE, TILE), 0)
    jj = lax.broadcasted_iota(jnp.int32, (TILE, TILE), 1)
    in_low = jj < feats
    take = [
        jnp.where((ii == jj + h * feats) & in_low, 1.0, 0.0).astype(jnp.bfloat16) for h in range(2)
    ]
    half_ones = [
        jnp.where((ii // feats) == h, 1.0, 0.0).astype(jnp.bfloat16) for h in range(2)
    ]

    def unpack_x(owner):
        def body(q, carry):
            v = xg[owner, pl.ds(pl.multiple_of(q * TILE, TILE), TILE), :]
            for h in range(2):
                xa[owner * rb + h * (rb // 2) + q] = mm(v, take[h], NN_DIMS).astype(jnp.bfloat16)
            return carry
        lax.fori_loop(0, rb // 2, body, 0)

    def unpack_y(owner):
        def body(q, carry):
            v = yg[owner, pl.ds(pl.multiple_of(q * TILE, TILE), TILE), :]
            wide = v.astype(jnp.float32)
            hi, lo = split2(wide * wide)
            for h in range(2):
                b = owner * cb + h * (cb // 2) + q
                ya[b] = mm(v, take[h], NN_DIMS).astype(jnp.bfloat16)
                norm = mm(hi, half_ones[h], NN_DIMS) + mm(lo, half_ones[h], NN_DIMS)
                ny[b] = norm * (0.5 * kappa)
            return carry
        lax.fori_loop(0, cb // 2, body, 0)

    unpack_x(t)
    unpack_y(s)
    x_copies[to_mate].wait()
    unpack_x(mate)
    forwards = {}
    for d in range(1, max(n_z, n_s)):
        if d < n_z:
            x_copies[d].wait_recv()
            forwards[d] = send_x(before(t, d), sem_f, d, mate)
            unpack_x(before(t, d))
        if d < n_s:
            y_copies[d].wait()
            unpack_y(lax.rem(s - d + n_s, n_s))
    for d in range(1, n_z):
        forwards[d].wait_recv()
        unpack_x(before(mate, d))
    for d in range(1, n_z):
        x_copies[d].wait_send()
        forwards[d].wait_send()
    for copy in small:
        copy.wait()
    for o in range(n_t):
        mass[pl.ds(o * rb, rb), :] = jnp.exp(lag[o])
    for o in range(n_s):
        lb_full[pl.ds(o * cb, cb), :] = lbg[o] * LOG2E

    unroll = 32

    def first_rows(g, carry):
        for q in range(unroll):
            k = g * unroll + q
            r = rows_s[k]
            c = cols_s[k]
            w = mm(ya[c], xa[r], NT_DIMS) * kappa - ny[c]
            m = jnp.max(w, axis=0, keepdims=True)
            slot_max[pl.ds(k, 1), :] = m
            slot_sum[pl.ds(k, 1), :] = jnp.sum(jnp.exp2(w - m), axis=0, keepdims=True)
        return carry

    def first_cols(g, carry):
        for q in range(unroll):
            k = g * unroll + q
            r = rows_s[k]
            c = cols_s[k]
            w = mm(xa[r], ya[c], NT_DIMS) * kappa + abc[r]
            m = jnp.max(w, axis=0, keepdims=True)
            e = jnp.exp2(w - m)
            slot_max[pl.ds(k, 1), :] = m
            slot_sum[pl.ds(k, 1), :] = jnp.sum(e, axis=0, keepdims=True)
            tiles[k] = e.astype(jnp.bfloat16)
        return carry

    group = 8

    def by_block(ids1, values):
        which = lax.broadcasted_iota(jnp.int32, (blocks, slots), 0)
        onehot = jnp.where(which == ids1, 1.0, 0.0).astype(jnp.bfloat16)
        hi, lo = split2(values)
        return mm(onehot, hi, NN_DIMS) + mm(onehot, lo, NN_DIMS)

    def combine_lse(ids, ids1):
        def body(g, carry):
            base = (g * group).astype(jnp.float32)
            tall = [jnp.full((8, TILE), LOW, jnp.float32)] * group
            for ch in range(slots // 8):
                at = slice(ch * 8, ch * 8 + 8)
                offset = ids[at, :] - base
                high = slot_max[at, :]
                for b in range(group):
                    tall[b] = jnp.maximum(tall[b], jnp.where(offset == b, high, LOW))
            for b in range(group):
                tops[pl.ds(g * group + b, 1), :] = jnp.max(tall[b], axis=0, keepdims=True)
            return carry
        lax.fori_loop(0, blocks // group, body, 0)
        top = tops[...]
        lane = lax.broadcasted_iota(jnp.int32, (slots, TILE), 1).astype(jnp.float32)
        pick = jnp.where(ids[...] == lane, 1.0, 0.0)[:, :blocks].astype(jnp.bfloat16)
        hi, rest = split2(top)
        rest = top - hi.astype(jnp.float32)
        mid, low = split2(rest)
        seen = mm(pick, hi, NN_DIMS) + mm(pick, mid, NN_DIMS) + mm(pick, low, NN_DIMS)
        scaled = slot_sum[...] * jnp.exp2(jnp.minimum(slot_max[...] - seen, 1.0))
        return top + log2(by_block(ids1, scaled))

    def lse_of(values):
        top = functools.reduce(jnp.maximum, values)
        return top + log2(sum(jnp.exp2(v - top) for v in values))

    lax.fori_loop(0, slots // unroll, first_rows, 0)
    lse = combine_lse(ridb, rid1)
    for o in range(n_t):
        row_part[o] = lse[o * rb:(o + 1) * rb, :]
    copies = [
        send(row_part.at[lax.rem(t + d, n_t)], row_recv.at[d], sem_ra, (d,), d, True)
        for d in range(1, n_t)
    ]
    for copy in copies:
        copy.wait()
    la2 = la_ref[...] * LOG2E
    a_first = la2 - lse_of([row_part[t]] + [row_recv[d] for d in range(1, n_t)])
    a_full[t] = a_first
    copies = [send(a_full.at[t], a_full.at[t], sem_rb, (d,), d, True) for d in range(1, n_t)]
    for copy in copies:
        copy.wait()
    for o in range(n_t):
        a_cur[pl.ds(o * rb, rb), :] = a_full[o]

    def spread(g, carry):
        for q in range(4):
            r = g * 4 + q
            abc[r] = jnp.transpose(jnp.broadcast_to(a_cur[pl.ds(r, 1), :], (TILE, TILE)))
        return carry
    lax.fori_loop(0, blocks // 4, spread, 0)

    lax.fori_loop(0, slots // unroll, first_cols, 0)
    col_part[...] = combine_lse(cidb, cid1)
    copies = [send(col_part, col_recv.at[d], sem_c, (0, d), d, False) for d in range(1, n_s)]
    for copy in copies:
        copy.wait()
    lse = lse_of([col_part[...]] + [col_recv[d] for d in range(1, n_s)])
    b_cur[...] = lb_full[...] - lse

    wide_unroll = 32

    def later_rows(g, carry):
        for q in range(wide_unroll):
            k = g * wide_unroll + q
            c = cols_s[k]
            w = jnp.exp2(jnp.minimum(slot_max[pl.ds(k, 1), :] + b_cur[pl.ds(c, 1), :], 100.0))
            got = mm(stack_hi_lo(w), tiles[k], NT_DIMS)
            slot_sum[pl.ds(k, 1), :] = got[0:1, :] + got[1:2, :]
        return carry

    def later_cols(g, carry):
        for q in range(wide_unroll):
            k = g * wide_unroll + q
            r = rows_s[k]
            c = cols_s[k]
            got = mm(stack_hi_lo(a_cur[pl.ds(r, 1), :]), tiles[k], NN_DIMS)
            f = jnp.exp2(jnp.minimum(slot_max[pl.ds(k, 1), :] + b_cur[pl.ds(c, 1), :], 60.0))
            slot_sum[pl.ds(k, 1), :] = (got[0:1, :] + got[1:2, :]) * f
        return carry

    def totals(own, sums, sums_in, sems, it, n, along_tgt):
        sums[it - 1] = own.astype(jnp.bfloat16)
        copies = [
            send(sums.at[it - 1], sums_in.at[it - 1, d], sems, (it, d), d, along_tgt)
            for d in range(1, n)
        ]
        for copy in copies:
            copy.wait()
        return own + sum(sums_in[it - 1, d].astype(jnp.float32) for d in range(1, n))

    for it in range(1, ITERS):
        lax.fori_loop(0, slots // wide_unroll, later_rows, 0)
        own = by_block(rid1, slot_sum[...])
        a_cur[...] = mass[...] / totals(own, row_sums, row_sums_in, sem_r, it, n_t, True)
        if it == ITERS - 1:
            a_out[...] = a_first + log2(a_cur[pl.ds(t * rb, rb), :])
        lax.fori_loop(0, slots // wide_unroll, later_cols, 0)
        own = by_block(cid1, slot_sum[...])
        if it < ITERS - 1:
            total = totals(own, col_sums, col_sums_in, sem_c, it, n_s, False)
            b_cur[...] = b_cur[...] + lb_full[...] - log2(total)
        else:
            for o in range(n_s):
                last_part[o] = own[o * cb:(o + 1) * cb, :]
            copies = [
                send(last_part.at[lax.rem(s + d, n_s)], last_in.at[d], sem_c, (it, d), d, False)
                for d in range(1, n_s)
            ]
            for copy in copies:
                copy.wait()
            total = last_part[s] + sum(last_in[d] for d in range(1, n_s))
            at = pl.ds(s * cb, cb)
            b_out[...] = b_cur[at, :] + lb_full[at, :] - log2(total)


def halves(points):
    half = points.shape[0] // 2
    return jnp.concatenate([points[:half], points[half:]], axis=1)


def local(n_s, n_t, sources, targets, log_src, log_tgt, tile_rows, tile_cols, tile_count):
    feats = sources.shape[1]
    slots = tile_rows.shape[-1]
    blocks = sources.shape[0] * n_t // TILE
    rb, cb = blocks // n_t, blocks // n_s
    rows = tile_rows.reshape(-1)
    cols = tile_cols.reshape(-1)
    vm = pl.BlockSpec(memory_space=pltpu.VMEM)
    sm = pl.BlockSpec(memory_space=pltpu.SMEM)
    f32, bf16, i32 = jnp.float32, jnp.bfloat16, jnp.int32
    dma = pltpu.SemaphoreType.DMA
    xp, yp = halves(sources), halves(targets)
    a_own, b_own = pl.pallas_call(
        functools.partial(kernel, n_s, n_t, blocks, slots, feats),
        out_shape=(
            jax.ShapeDtypeStruct((rb, TILE), f32),
            jax.ShapeDtypeStruct((cb, TILE), f32),
        ),
        in_specs=[sm] * 3 + [vm] * 6,
        out_specs=(vm, vm),
        scratch_shapes=[
            pltpu.VMEM((n_t, *xp.shape), bf16),
            pltpu.VMEM((n_s, *yp.shape), bf16),
            pltpu.VMEM((n_t, rb, TILE), f32),
            pltpu.VMEM((n_s, cb, TILE), f32),
            pltpu.VMEM((blocks, TILE, TILE), bf16),
            pltpu.VMEM((blocks, TILE, TILE), bf16),
            pltpu.VMEM((blocks, TILE, TILE), f32),
            pltpu.VMEM((blocks, TILE, TILE), f32),
            pltpu.VMEM((slots, TILE, TILE), bf16),
            pltpu.VMEM((slots, TILE), f32),
            pltpu.VMEM((slots, TILE), f32),
            pltpu.VMEM((slots, TILE), f32),
            pltpu.VMEM((slots, TILE), f32),
            pltpu.VMEM((blocks, TILE), f32),
            pltpu.VMEM((n_t, rb, TILE), f32),
            pltpu.VMEM((n_t, rb, TILE), f32),
            pltpu.VMEM((n_t, rb, TILE), f32),
            pltpu.VMEM((blocks, TILE), f32),
            pltpu.VMEM((blocks, TILE), f32),
            pltpu.VMEM((n_s, blocks, TILE), f32),
            pltpu.VMEM((blocks, TILE), f32),
            pltpu.VMEM((blocks, TILE), f32),
            pltpu.VMEM((blocks, TILE), f32),
            pltpu.VMEM((ITERS - 1, blocks, TILE), bf16),
            pltpu.VMEM((ITERS - 1, n_t, blocks, TILE), bf16),
            pltpu.VMEM((ITERS - 1, blocks, TILE), bf16),
            pltpu.VMEM((ITERS - 1, n_s, blocks, TILE), bf16),
            pltpu.VMEM((n_s, cb, TILE), f32),
            pltpu.VMEM((n_s, cb, TILE), f32),
            dma((2, n_t)),
            dma((2, n_t)),
            dma((2, n_s)),
            dma((2, n_t)),
            dma((2, n_s)),
            dma((2, n_t)),
            dma((2, n_t)),
            dma((2, ITERS, n_t)),
            dma((2, ITERS, n_s)),
        ],
        compiler_params=pltpu.CompilerParams(
            collective_id=0, has_side_effects=True, vmem_limit_bytes=48 * 2**20
        ),
        cost_estimate=pl.CostEstimate(
            flops=12 * slots * TILE**3, bytes_accessed=2**20, transcendentals=2 * slots * TILE**2
        ),
    )(
        rows, cols, tile_count, rows.reshape(1, -1), cols.reshape(1, -1),
        xp, yp, log_src.reshape(rb, TILE), log_tgt.reshape(cb, TILE),
    )
    scale = EPS_BLUR / LOG2E
    return tuple(
        own.reshape(-1) * scale + jnp.sum(points.astype(f32) ** 2, axis=-1) * (1.0 / feats)
        for own, points in ((a_own, sources), (b_own, targets))
    )


def solution(mesh):
    in_specs = (
        P(("src", "tgt"), None),
        P(("src", "tgt"), None),
        P(("src", "tgt")),
        P(("src", "tgt")),
        P("src", "tgt", None),
        P("src", "tgt", None),
        P("src", "tgt"),
    )
    out_specs = (P(("src", "tgt")), P(("src", "tgt")))
    body = functools.partial(local, mesh.shape["src"], mesh.shape["tgt"])
    return jax.shard_map(body, mesh=mesh, in_specs=in_specs, out_specs=out_specs, check_vma=False)
```
